32 devices in a mesh: rows: 16 (over z, y, x), cols: 2 (over core).
Axes of the slice: x: 2, y: 2, z: 4, core: 2. Of those that a mesh axis runs over, the one named last changes fastest.
Arguments:
- deviations: float32 [12288, 8192], P('rows', 'cols')
- test_signs: int32 [8192, 128], P('cols'), may hold values from -1 to 1, as said below
Outputs:
- basis: float32 [12288, 128], P('rows')
- projected: float32 [128, 8192], P('rows', 'cols')
The draws below stay inside these ranges and needn't reach their ends.
Inputs may be any that keep to these rules, and one draw needn't show every extreme that they name: `test_signs`: every entry is -1 or 1.
All inputs are finite; a program needn't handle non-finite values.
Results may differ from the reference program's by a relative error of at most 0.0003.
Values sent between devices are 32-bit elements; how exact they have to be, the bound alone decides.
No kernel may reach another device: no remote copies, remote signals or barrier semaphores. Data moves between devices by JAX's collectives and lax.ppermute only.
A program may use at most 64 MiB of HBM per device.

```python
import math
import jax
import jax.numpy as jnp
from jax import lax

SCANS = 8192
RANK = 128
SAMPLES = 12288


def draw_deviations(key, part):
    keys = jax.random.split(key, 3)
    positions = jnp.arange(SAMPLES, dtype=jnp.float32)
    rising = 1.0 + 2.0 * positions / SAMPLES
    row_scale = jnp.exp(jax.random.uniform(keys[0], (SAMPLES,), jnp.float32) * math.log(10.0)) * rising
    col_scale = jnp.exp(jax.random.uniform(keys[1], (SCANS,), jnp.float32) * math.log(10.0))
    noise = jax.random.normal(keys[2], (SAMPLES, SCANS), jnp.float32)
    return (noise * row_scale[:, None] * col_scale[None, :] / 16.0).astype(jnp.float32)


def draw_test_signs(key, part):
    coins = jax.random.randint(key, (SCANS, RANK), 0, 2, jnp.int32)
    return (2 * coins - 1).astype(jnp.int32)


def setup_inputs(seed: int = 0) -> dict:
    key_of = jax.random.split(jax.random.key(seed), 3)
    deviations = draw_deviations(jax.random.fold_in(key_of[2], 71), 0)
    test_signs = draw_test_signs(jax.random.fold_in(key_of[2], 71), 0)
    return dict(deviations=deviations, test_signs=test_signs)


def reference(deviations, test_signs):
    test_matrix = test_signs.astype(jnp.float32) / math.sqrt(SCANS)
    sketch = jnp.dot(deviations.astype(jnp.float32), test_matrix.astype(jnp.float32), precision=lax.Precision.HIGHEST, preferred_element_type=jnp.float32)
    orthonormal, factor = jnp.linalg.qr(sketch)
    signs = jnp.sign(jnp.diagonal(factor))
    orthonormal = orthonormal * signs[None, :]
    basis = orthonormal * math.sqrt(SAMPLES)
    projected = jnp.dot(orthonormal.T.astype(jnp.float32), deviations.astype(jnp.float32), precision=lax.Precision.HIGHEST, preferred_element_type=jnp.float32)
    return (basis, projected)
```

```python
import functools
import math

import jax
import jax.numpy as jnp
from jax import lax
from jax.experimental import pallas as pl
from jax.experimental.pallas import tpu as pltpu
from jax.sharding import PartitionSpec as P

SCANS = 8192

precise = lax.Precision.HIGHEST
MIB = 1 << 20


def split(value):
    high = value.astype(jnp.bfloat16)
    low = (value - high.astype(jnp.float32)).astype(jnp.bfloat16)
    return high, low


def dot(a, b):
    return jnp.dot(a, b, preferred_element_type=jnp.float32)


def vmem():
    return pl.BlockSpec(memory_space=pltpu.VMEM)


def params(mib=40):
    return pltpu.CompilerParams(vmem_limit_bytes=mib * MIB)


def sketch_kernel(unit, gain, dev_ref, sign_ref, out_ref):
    step = pl.program_id(0)
    omega = (sign_ref[...].astype(jnp.float32) * unit).astype(jnp.bfloat16)
    high, low = split(dev_ref[...])
    part = dot(high, omega) + dot(low, omega)

    @pl.when(step == 0)
    def _():
        out_ref[...] = part

    @pl.when(step > 0)
    def _():
        out_ref[...] += part

    @pl.when(step == pl.num_programs(0) - 1)
    def _():
        out_ref[...] *= gain


def sketch_of(dev, signs):
    rows, cols = dev.shape
    rank = signs.shape[1]
    block = min(512, cols)
    unit = 2.0 ** -math.ceil(math.log2(math.sqrt(SCANS)))
    gain = 1.0 / (math.sqrt(SCANS) * unit)
    return pl.pallas_call(
        functools.partial(sketch_kernel, unit, gain),
        grid=(cols // block,),
        in_specs=[
            pl.BlockSpec((rows, block), lambda i: (0, i)),
            pl.BlockSpec((block, rank), lambda i: (i, 0)),
        ],
        out_specs=pl.BlockSpec((rows, rank), lambda i: (0, 0)),
        out_shape=jax.ShapeDtypeStruct((rows, rank), jnp.float32),
        compiler_params=params(),
    )(dev, signs)


def gram_kernel(parts, *refs):
    total_ref, pair_ref, gram_ref = refs[parts:]
    total = refs[0][...]
    for ref in refs[1:parts]:
        total = total + ref[...]
    total_ref[...] = total
    flat = total.T
    high, low = split(flat)
    rank = flat.shape[0]
    pair_ref[:rank, :] = high
    pair_ref[rank:, :] = low
    gram_ref[...] = lax.dot_general(
        flat, total, (((1,), (0,)), ((), ())),
        precision=precise, preferred_element_type=jnp.float32,
    )


def gram_of(*sketches):
    rows, rank = sketches[0].shape
    return pl.pallas_call(
        functools.partial(gram_kernel, len(sketches)),
        in_specs=[vmem()] * len(sketches),
        out_specs=[vmem()] * 3,
        out_shape=[
            jax.ShapeDtypeStruct((rows, rank), jnp.float32),
            jax.ShapeDtypeStruct((2 * rank, rows), jnp.bfloat16),
            jax.ShapeDtypeStruct((rank, rank), jnp.float32),
        ],
        compiler_params=params(),
    )(*sketches)


def cross_kernel(steps, index_ref, pair_ref, dev_ref, first_ref, second_ref):
    step = pl.program_id(0)
    rank = first_ref.shape[0]
    high, low = split(dev_ref[...])
    both = dot(pair_ref[...], high)
    value = (both[:rank] + both[rank:]) + dot(pair_ref[:rank, :], low)

    @pl.when(step < steps)
    def _():
        first_ref[...] = value

    @pl.when(step >= steps)
    def _():
        second_ref[...] = value


def cross_of(index, pair, dev, width):
    rank, rows = pair.shape[0] // 2, pair.shape[1]
    block = min(512, width)
    steps = width // block

    def dev_map(i, index_ref):
        return (0, index_ref[i // steps] * steps + i % steps)

    return pl.pallas_call(
        functools.partial(cross_kernel, steps),
        grid_spec=pltpu.PrefetchScalarGridSpec(
            num_scalar_prefetch=1,
            grid=(2 * steps,),
            in_specs=[
                pl.BlockSpec((2 * rank, rows), lambda i, index_ref: (0, 0)),
                pl.BlockSpec((rows, block), dev_map),
            ],
            out_specs=[
                pl.BlockSpec((rank, block), lambda i, index_ref: (0, jnp.minimum(i, steps - 1))),
                pl.BlockSpec((rank, block), lambda i, index_ref: (0, jnp.maximum(i - steps, 0))),
            ],
        ),
        out_shape=[jax.ShapeDtypeStruct((rank, width), jnp.float32)] * 2,
        compiler_params=params(),
    )(index, pair, dev)


def project_kernel(groups, index_ref, inverse_ref, a_ref, b_ref, c_ref, d_ref, *outs):
    group = outs[0].shape[0]
    half = a_ref.shape[1]
    left = a_ref[...] + b_ref[...]
    right = c_ref[...] + d_ref[...]
    for k in range(groups):
        start = pl.multiple_of((index_ref[0] ^ k) * group, group)
        factor = inverse_ref[pl.ds(start, group), :]
        outs[k][:, :half] = jnp.dot(factor, left, precision=precise, preferred_element_type=jnp.float32)
        outs[k][:, half:] = jnp.dot(factor, right, precision=precise, preferred_element_type=jnp.float32)


def project(index, inverse, parts, groups):
    rank, half = parts[0].shape
    shape = jax.ShapeDtypeStruct((rank // groups, 2 * half), jnp.float32)
    return pl.pallas_call(
        functools.partial(project_kernel, groups),
        in_specs=[pl.BlockSpec(memory_space=pltpu.SMEM)] + [vmem()] * 5,
        out_specs=[vmem()] * groups,
        out_shape=[shape] * groups,
        compiler_params=params(),
    )(index, inverse, *parts)


def local(deviations, test_signs):
    rows, cols = deviations.shape
    n, n_cols = lax.axis_size("rows"), lax.axis_size("cols")
    samples = rows * n
    me = lax.axis_index("rows")
    x, y, z = me & 1, (me >> 1) & 1, me >> 2
    n_z = n // 4

    def swap(value, bit):
        return lax.ppermute(value, "rows", [(i, i ^ bit) for i in range(n)])

    part = sketch_of(deviations, test_signs)
    step = 1
    while 2 * step < n_cols:
        part = part + lax.ppermute(part, "cols", [(i, i ^ step) for i in range(n_cols)])
        step *= 2
    other = lax.ppermute(part, "cols", [(i, i ^ step) for i in range(n_cols)])
    sketch, pair, gram = gram_of(part, other)

    step = 1
    while step < n:
        gram = gram + swap(gram, step)
        step *= 2

    width = cols // 4
    away = jnp.stack([1 - x, 3 - y]).astype(jnp.int32)
    home = jnp.stack([x, 2 + y]).astype(jnp.int32)
    send_x, send_y = cross_of(away, pair, deviations, width)
    got_x, got_y = swap(send_x, 1), swap(send_y, 2)
    keep_x, keep_y = cross_of(home, pair, deviations, width)
    half = width // 2

    def cut(value, which):
        return lax.dynamic_slice_in_dim(value, which * half, half, 1)

    next_x = cut(keep_x, 1 - y) + cut(got_x, 1 - y)
    next_y = cut(keep_y, 1 - x) + cut(got_y, 1 - x)
    last_x = cut(keep_x, y) + cut(got_x, y)
    last_y = cut(keep_y, x) + cut(got_y, x)
    then_x, then_y = swap(next_x, 2), swap(next_y, 1)

    low = jnp.linalg.cholesky(gram)
    inverse = jax.scipy.linalg.solve_triangular(low, jnp.eye(gram.shape[0], dtype=jnp.float32), lower=True)

    groups = project(z[None], inverse, (last_x, then_x, last_y, then_y), n_z)
    total = groups[0]
    for k in range(1, n_z):
        total = total + swap(groups[k], 4 * k)

    each = total.shape[0] // 4
    mine = me & 3
    found = []
    for k in range(4):
        block = lax.dynamic_slice_in_dim(total, (mine ^ k) * each, each, 0)
        found.append(swap(block, k) if k else block)
    for bit in (1, 2):
        flip = (mine & bit) != 0
        found = [jnp.where(flip, found[k ^ bit], found[k]) for k in range(4)]
    projected = jnp.concatenate(
        [found[k][:, :half] for k in (0, 2, 1, 3)] + [found[k][:, half:] for k in (0, 1, 2, 3)], axis=1
    )

    basis = lax.dot_general(
        sketch, inverse, (((1,), (1,)), ((), ())),
        precision=precise, preferred_element_type=jnp.float32,
    ) * math.sqrt(samples)
    return (basis, projected)


def solution(mesh):
    return jax.shard_map(
        local,
        mesh=mesh,
        in_specs=(P("rows", "cols"), P("cols", None)),
        out_specs=(P("rows", None), P("rows", "cols")),
        check_vma=False,
    )
```

```python
import functools
import math

import jax
import jax.numpy as jnp
from jax import lax
from jax.experimental import pallas as pl
from jax.experimental.pallas import tpu as pltpu
from jax.sharding import PartitionSpec as P

SCANS = 8192

precise = lax.Precision.HIGHEST
MIB = 1 << 20


def split(value):
    high = value.astype(jnp.bfloat16)
    low = (value - high.astype(jnp.float32)).astype(jnp.bfloat16)
    return high, low


def dot(a, b):
    return jnp.dot(a, b, preferred_element_type=jnp.float32)


def vmem():
    return pl.BlockSpec(memory_space=pltpu.VMEM)


def place():
    me = lax.axis_index("rows")
    return me & 1, (me >> 1) & 1, me


def params(mib):
    return pltpu.CompilerParams(vmem_limit_bytes=mib * MIB)


def sketch_kernel(unit, gain, depth, dev_hbm, sign_hbm, high_ref, low_ref, out_ref, dev_buf, sign_buf, omega, dev_sem, sign_sem):
    block = dev_buf.shape[1]
    steps = high_ref.shape[0] // block
    signs = pltpu.make_async_copy(sign_hbm, sign_buf, sign_sem)
    signs.start()

    def fetch(i):
        return pltpu.make_async_copy(
            dev_hbm.at[pl.ds(i * block, block), :], dev_buf.at[i % depth], dev_sem.at[i % depth]
        )

    for i in range(min(depth - 1, steps)):
        fetch(i).start()
    signs.wait()
    omega[...] = (sign_buf[...].astype(jnp.float32) * unit).astype(jnp.bfloat16)
    for i in range(steps):
        if i + depth - 1 < steps:
            fetch(i + depth - 1).start()
        fetch(i).wait()
        here = slice(i * block, (i + 1) * block)
        high, low = split(dev_buf[i % depth])
        high_ref[here, :] = high
        low_ref[here, :] = low
        out_ref[here, :] = (dot(high, omega[...]) + dot(low, omega[...])) * gain


def sketch_of(dev, signs):
    rows, cols = dev.shape
    rank = signs.shape[1]
    block, depth = rows // 4, 3
    unit = 2.0 ** -math.ceil(math.log2(math.sqrt(SCANS)))
    gain = 1.0 / (math.sqrt(SCANS) * unit)
    dev = pltpu.with_memory_space_constraint(dev, pltpu.HBM)
    signs = pltpu.with_memory_space_constraint(signs, pltpu.HBM)
    return pl.pallas_call(
        functools.partial(sketch_kernel, unit, gain, depth),
        in_specs=[pl.BlockSpec(memory_space=pltpu.HBM)] * 2,
        out_specs=[vmem()] * 3,
        out_shape=[pltpu.VMEM((rows, cols), jnp.bfloat16)] * 2 + [pltpu.VMEM((rows, rank), jnp.float32)],
        scratch_shapes=[
            pltpu.VMEM((depth, block, cols), jnp.float32),
            pltpu.VMEM((cols, rank), jnp.int32),
            pltpu.VMEM((cols, rank), jnp.bfloat16),
            pltpu.SemaphoreType.DMA((depth,)),
            pltpu.SemaphoreType.DMA,
        ],
        compiler_params=params(24),
        name="sketch",
    )(dev, signs)


def gram_kernel(parts, *refs):
    total_ref, pair_ref, gram_ref = refs[parts:]
    total = refs[0][...]
    for ref in refs[1:parts]:
        total = total + ref[...]
    total_ref[...] = total
    flat = total.T
    high, low = split(flat)
    rank = flat.shape[0]
    pair_ref[:rank, :] = high
    pair_ref[rank:, :] = low
    gram_ref[...] = lax.dot_general(
        flat, total, (((1,), (0,)), ((), ())),
        precision=precise, preferred_element_type=jnp.float32,
    )


def gram_of(*sketches):
    rows, rank = sketches[0].shape
    return pl.pallas_call(
        functools.partial(gram_kernel, len(sketches)),
        in_specs=[vmem()] * len(sketches),
        out_specs=[vmem()] * 3,
        out_shape=[
            jax.ShapeDtypeStruct((rows, rank), jnp.float32),
            jax.ShapeDtypeStruct((2 * rank, rows), jnp.bfloat16),
            jax.ShapeDtypeStruct((rank, rank), jnp.float32),
        ],
        compiler_params=params(8),
        name="gram",
    )(*sketches)


def cross_kernel(block, stay, pair_ref, high_ref, low_ref, *outs):
    rank, width = outs[0].shape
    x, y = place()[:2]
    chunks = (x, 2 + y) if stay else (1 - x, 3 - y)
    for chunk, out in zip(chunks, outs):
        for t in range(width // block):
            start = pl.multiple_of(chunk * width + t * block, 128)
            high = high_ref[:, pl.ds(start, block)]
            low = low_ref[:, pl.ds(start, block)]
            both = dot(pair_ref[...], high)
            out[:, t * block:(t + 1) * block] = (both[:rank] + both[rank:]) + dot(pair_ref[:rank, :], low)


def cross_of(stay, pair, high, low):
    rank, rows = pair.shape[0] // 2, pair.shape[1]
    width = high.shape[1] // 4
    return pl.pallas_call(
        functools.partial(cross_kernel, min(512, width), stay),
        in_specs=[vmem()] * 3,
        out_specs=[vmem()] * 2,
        out_shape=[jax.ShapeDtypeStruct((rank, width), jnp.float32)] * 2,
        compiler_params=params(8),
        cost_estimate=pl.CostEstimate(flops=12 * rank * rows * width, bytes_accessed=8 * rows * width, transcendentals=0),
        name="cross_stay" if stay else "cross_leave",
    )(pair, high, low)


def thirds(value):
    high = value.astype(jnp.bfloat16)
    rest = value - high.astype(jnp.float32)
    middle = rest.astype(jnp.bfloat16)
    low = (rest - middle.astype(jnp.float32)).astype(jnp.bfloat16)
    return high, middle, low


def inverse_kernel(gram_ref, out_ref, work):
    rank = gram_ref.shape[0]
    rows = lax.broadcasted_iota(jnp.int32, (rank, rank), 0)
    lanes = lax.broadcasted_iota(jnp.int32, (rank, rank), 1)
    work[:, :rank] = gram_ref[...]
    work[:, rank:] = jnp.where(rows == lanes, 1.0, 0.0)
    for base in range(0, rank, 8):
        left = work[base:base + 8, :rank]
        block = {}
        for j in range(8):
            column = jnp.broadcast_to(left[:, base + j:base + j + 1], (8, rank))
            for i in range(j, 8):
                block[i, j] = column[i:i + 1, :]
        a = [work[base + i:base + i + 1, :rank] for i in range(8)]
        e = [work[base + i:base + i + 1, rank:] for i in range(8)]
        for j in range(8):
            scale = lax.rsqrt(block[j, j])
            a[j] = a[j] * scale
            e[j] = e[j] * scale
            factor = {i: block[i, j] * scale for i in range(j + 1, 8)}
            for i in range(j + 1, 8):
                for k in range(j + 1, i + 1):
                    block[i, k] = block[i, k] - factor[i] * factor[k]
                a[i] = a[i] - factor[i] * a[j]
                e[i] = e[i] - factor[i] * e[j]
            work[base + j:base + j + 1, :rank] = a[j]
            work[base + j:base + j + 1, rank:] = e[j]
        if base + 8 < rank:
            high, middle, low = thirds(work[base:base + 8, :])
            first = jnp.concatenate([high, high, middle, middle, high, low], axis=0)[:, :rank]
            second = jnp.concatenate([high, middle, high, middle, low, high], axis=0)
            update = lax.dot_general(
                first, second, (((0,), (0,)), ((), ())), preferred_element_type=jnp.float32
            )
            work[base + 8:, :] = work[base + 8:, :] - update[base + 8:, :]
    out_ref[...] = jnp.where(lanes <= rows, work[:, rank:], 0.0)


def inverse_of(gram):
    rank = gram.shape[0]
    return pl.pallas_call(
        inverse_kernel,
        in_specs=[vmem()],
        out_specs=vmem(),
        out_shape=jax.ShapeDtypeStruct((rank, rank), jnp.float32),
        scratch_shapes=[pltpu.VMEM((rank, 2 * rank), jnp.float32)],
        compiler_params=params(8),
        cost_estimate=pl.CostEstimate(flops=8 * 10**9, bytes_accessed=10**6, transcendentals=0),
        name="inverse",
    )(gram)


def onward_kernel(axis, keep_ref, got_ref, out_ref):
    half = out_ref.shape[1]
    here = pl.ds(pl.multiple_of((1 - place()[axis]) * half, 128), half)
    out_ref[...] = keep_ref[:, here] + got_ref[:, here]


def onward(axis, keep, got):
    rank, width = keep.shape
    return pl.pallas_call(
        functools.partial(onward_kernel, axis),
        in_specs=[vmem()] * 2,
        out_specs=vmem(),
        out_shape=jax.ShapeDtypeStruct((rank, width // 2), jnp.float32),
        compiler_params=params(8),
        name="onward",
    )(keep, got)


def project_kernel(n, inverse_ref, keep_x, got_x, then_x, keep_y, got_y, then_y, *refs):
    outs, ordered = refs[:-1], refs[-1]
    group, half = outs[0].shape[0], then_x.shape[1]
    each = ordered.shape[0] // n
    x, y, me = place()
    for i in range(n):
        ordered[i * each:(i + 1) * each, :] = inverse_ref[pl.ds((me ^ i) * each, each), :]
    at_x = pl.ds(pl.multiple_of(y * half, 128), half)
    at_y = pl.ds(pl.multiple_of(x * half, 128), half)
    left = (keep_x[:, at_x] + got_x[:, at_x]) + then_x[...]
    right = (keep_y[:, at_y] + got_y[:, at_y]) + then_y[...]
    left = jnp.dot(ordered[...], left, precision=precise, preferred_element_type=jnp.float32)
    right = jnp.dot(ordered[...], right, precision=precise, preferred_element_type=jnp.float32)
    for k, out in enumerate(outs):
        out[:, :half] = left[k * group:(k + 1) * group]
        out[:, half:] = right[k * group:(k + 1) * group]


def project(n, inverse, *parts):
    rank, half = parts[2].shape
    groups = n // 4
    shape = jax.ShapeDtypeStruct((rank // groups, 2 * half), jnp.float32)
    return pl.pallas_call(
        functools.partial(project_kernel, n),
        in_specs=[vmem()] * 7,
        out_specs=[vmem()] * groups,
        out_shape=[shape] * groups,
        scratch_shapes=[pltpu.VMEM((rank, rank), jnp.float32)],
        compiler_params=params(8),
        name="project",
    )(inverse, *parts)


def collect_kernel(parts, *refs):
    outs = refs[parts:]
    each = outs[0].shape[0]
    for k, out in enumerate(outs):
        total = refs[0][k * each:(k + 1) * each, :]
        for ref in refs[1:parts]:
            total = total + ref[k * each:(k + 1) * each, :]
        out[...] = total


def collect(*parts):
    group, width = parts[0].shape
    return pl.pallas_call(
        functools.partial(collect_kernel, len(parts)),
        in_specs=[vmem()] * len(parts),
        out_specs=[vmem()] * 4,
        out_shape=[jax.ShapeDtypeStruct((group // 4, width), jnp.float32)] * 4,
        compiler_params=params(8),
        name="collect",
    )(*parts)


def assemble_kernel(*refs):
    out = refs[-1]
    half = out.shape[1] // 8
    x, y = place()[:2]
    for k, ref in enumerate(refs[:-1]):
        qx, qy = x ^ (k & 1), y ^ (k >> 1)
        out[:, pl.ds(pl.multiple_of((2 * qx + qy) * half, 128), half)] = ref[:, :half]
        out[:, pl.ds(pl.multiple_of((4 + 2 * qy + qx) * half, 128), half)] = ref[:, half:]


def assemble(*blocks):
    each, width = blocks[0].shape
    return pl.pallas_call(
        assemble_kernel,
        in_specs=[vmem()] * 4,
        out_specs=vmem(),
        out_shape=jax.ShapeDtypeStruct((each, 4 * width), jnp.float32),
        compiler_params=params(8),
        name="assemble",
    )(*blocks)


def local(deviations, test_signs):
    rows, cols = deviations.shape
    n, n_cols = lax.axis_size("rows"), lax.axis_size("cols")
    samples = rows * n

    def swap(value, bit):
        return lax.ppermute(value, "rows", [(i, i ^ bit) for i in range(n)])

    high, low, part = sketch_of(deviations, test_signs)
    step = 1
    while 2 * step < n_cols:
        part = part + lax.ppermute(part, "cols", [(i, i ^ step) for i in range(n_cols)])
        step *= 2
    other = lax.ppermute(part, "cols", [(i, i ^ step) for i in range(n_cols)])
    sketch, pair, gram = gram_of(part, other)

    leave = cross_of(False, pair, high, low)
    stay = cross_of(True, pair, high, low)

    step, beside = 1, [leave, stay]
    while step < n:
        found = [swap(gram, step * k) for k in range(1, min(4, n // step))]
        if beside:
            found, _ = lax.optimization_barrier((found, beside.pop(0)))
        for value in found:
            gram = gram + value
        step *= 4
    inverse = inverse_of(gram)

    got_x, got_y = swap(leave[0], 1), swap(leave[1], 2)
    then_x = swap(onward(1, stay[0], got_x), 2)
    then_y = swap(onward(0, stay[1], got_y), 1)

    groups = project(n, inverse, stay[0], got_x, then_x, stay[1], got_y, then_y)
    basis = lax.dot_general(
        sketch, inverse, (((1,), (1,)), ((), ())),
        precision=precise, preferred_element_type=jnp.float32,
    ) * math.sqrt(samples)
    found = [swap(groups[k], 4 * k) for k in range(1, n // 4)]
    found, basis = lax.optimization_barrier((found, basis))

    blocks = collect(groups[0], *found)
    blocks = [blocks[0]] + [swap(blocks[k], k) for k in range(1, 4)]
    return (basis, assemble(*blocks))


def solution(mesh):
    return jax.shard_map(
        local,
        mesh=mesh,
        in_specs=(P("rows", "cols"), P("cols", None)),
        out_specs=(P("rows", None), P("rows", "cols")),
        check_vma=False,
    )
```

```python
import functools
import math

import jax
import jax.numpy as jnp
from jax import lax
from jax.experimental import pallas as pl
from jax.experimental.pallas import tpu as pltpu
from jax.sharding import PartitionSpec as P

SCANS = 8192

precise = lax.Precision.HIGHEST
MIB = 1 << 20
little = pl.CostEstimate(flops=1000, bytes_accessed=1000, transcendentals=0)


def split(value):
    high = value.astype(jnp.bfloat16)
    low = (value - high.astype(jnp.float32)).astype(jnp.bfloat16)
    return high, low


def dot(a, b):
    return jnp.dot(a, b, preferred_element_type=jnp.float32)


def vmem():
    return pl.BlockSpec(memory_space=pltpu.VMEM)


def place():
    me = lax.axis_index("rows")
    return me & 1, (me >> 1) & 1, me


def params(mib):
    return pltpu.CompilerParams(vmem_limit_bytes=mib * MIB)


def sketch_kernel(unit, gain, steps, depth, dev_hbm, sign_hbm, dev_ref, out_ref, sign_buf, omega, dev_sem, sign_sem):
    block = dev_ref.shape[0] // steps
    signs = pltpu.make_async_copy(sign_hbm, sign_buf, sign_sem)
    signs.start()

    def fetch(i):
        here = pl.ds(i * block, block)
        return pltpu.make_async_copy(dev_hbm.at[here, :], dev_ref.at[here, :], dev_sem.at[i])

    for i in range(depth - 1):
        fetch(i).start()
    signs.wait()
    omega[...] = (sign_buf[...].astype(jnp.float32) * unit).astype(jnp.bfloat16)
    for i in range(steps):
        if i + depth - 1 < steps:
            fetch(i + depth - 1).start()
        fetch(i).wait()
        here = slice(i * block, (i + 1) * block)
        high, low = split(dev_ref[here, :])
        out_ref[here, :] = (dot(high, omega[...]) + dot(low, omega[...])) * gain


def sketch_of(dev, signs):
    rows, cols = dev.shape
    rank = signs.shape[1]
    steps, depth = 4, 3
    unit = 2.0 ** -math.ceil(math.log2(math.sqrt(SCANS)))
    gain = 1.0 / (math.sqrt(SCANS) * unit)
    dev = pltpu.with_memory_space_constraint(dev, pltpu.HBM)
    signs = pltpu.with_memory_space_constraint(signs, pltpu.HBM)
    return pl.pallas_call(
        functools.partial(sketch_kernel, unit, gain, steps, depth),
        in_specs=[pl.BlockSpec(memory_space=pltpu.HBM)] * 2,
        out_specs=[vmem()] * 2,
        out_shape=[pltpu.VMEM((rows, cols), jnp.float32), pltpu.VMEM((rows, rank), jnp.float32)],
        scratch_shapes=[
            pltpu.VMEM((cols, rank), jnp.int32),
            pltpu.VMEM((cols, rank), jnp.bfloat16),
            pltpu.SemaphoreType.DMA((steps,)),
            pltpu.SemaphoreType.DMA,
        ],
        compiler_params=params(24),
        name="sketch",
    )(dev, signs)


def join_kernel(parts, *refs):
    total_ref, pair_ref = refs[parts:]
    total = refs[0][...]
    for ref in refs[1:parts]:
        total = total + ref[...]
    total_ref[...] = total
    high, low = split(total.T)
    rank = high.shape[0]
    pair_ref[:rank, :] = high
    pair_ref[rank:, :] = low


def join(*sketches):
    rows, rank = sketches[0].shape
    return pl.pallas_call(
        functools.partial(join_kernel, len(sketches)),
        in_specs=[vmem()] * len(sketches),
        out_specs=[vmem()] * 2,
        out_shape=[
            jax.ShapeDtypeStruct((rows, rank), jnp.float32),
            jax.ShapeDtypeStruct((2 * rank, rows), jnp.bfloat16),
        ],
        compiler_params=params(8),
        name="join",
    )(*sketches)


def places(shape):
    return lax.broadcasted_iota(jnp.int32, shape, 0), lax.broadcasted_iota(jnp.int32, shape, 1)


def gram_kernel(tall_ref, packed_ref):
    tall = tall_ref[...]
    gram = lax.dot_general(
        tall, tall, (((0,), (0,)), ((), ())),
        precision=precise, preferred_element_type=jnp.float32,
    )
    half = gram.shape[0] // 2
    last = pltpu.roll(gram[half:], half, 1)
    rows, lanes = places(last.shape)
    packed_ref[:half, :] = jnp.where(rows <= lanes, gram[:half], last)
    diagonal = jnp.sum(jnp.where(rows == lanes, last, 0.0), axis=0, keepdims=True)
    packed_ref[half:, :] = jnp.broadcast_to(diagonal, (8, last.shape[1]))


def gram_of(tall):
    rank = tall.shape[1]
    return pl.pallas_call(
        gram_kernel,
        in_specs=[vmem()],
        out_specs=vmem(),
        out_shape=jax.ShapeDtypeStruct((rank // 2 + 8, rank), jnp.float32),
        compiler_params=params(8),
        cost_estimate=little,
        name="gram",
    )(tall)


def cross_kernel(block, stay, pair_ref, dev_ref, *outs):
    rank, width = outs[0].shape
    x, y = place()[:2]
    chunks = (x, 2 + y) if stay else (1 - x, 3 - y)
    for chunk, out in zip(chunks, outs):
        for t in range(width // block):
            start = pl.multiple_of(chunk * width + t * block, 128)
            high, low = split(dev_ref[:, pl.ds(start, block)])
            both = dot(pair_ref[...], high)
            out[:, t * block:(t + 1) * block] = (both[:rank] + both[rank:]) + dot(pair_ref[:rank, :], low)


def cross_of(stay, pair, dev):
    rank, rows = pair.shape[0] // 2, pair.shape[1]
    width = dev.shape[1] // 4
    return pl.pallas_call(
        functools.partial(cross_kernel, min(512, width), stay),
        in_specs=[vmem()] * 2,
        out_specs=[vmem()] * 2,
        out_shape=[jax.ShapeDtypeStruct((rank, width), jnp.float32)] * 2,
        compiler_params=params(8),
        cost_estimate=little,
        name="cross_stay" if stay else "cross_leave",
    )(pair, dev)


def thirds(value):
    high = value.astype(jnp.bfloat16)
    rest = value - high.astype(jnp.float32)
    middle = rest.astype(jnp.bfloat16)
    low = (rest - middle.astype(jnp.float32)).astype(jnp.bfloat16)
    return high, middle, low


def inverse_kernel(packed_ref, out_ref, work):
    rank = packed_ref.shape[1]
    half = rank // 2
    packed = packed_ref[:half, :]
    rows, lanes = places(packed.shape)
    corner = jnp.where(lanes < half, packed, 0.0)
    turned = jnp.concatenate([corner, jnp.zeros_like(corner)], axis=0).T[:half]
    work[:half, :rank] = jnp.where(rows <= lanes, packed, turned)
    last = jnp.where(rows > lanes, packed, jnp.where(rows < lanes, turned, packed_ref[half:half + 1, :]))
    work[half:, :rank] = jnp.where(lanes < half, 0.0, pltpu.roll(last, half, 1))
    rows, lanes = places((rank, rank))
    work[:, rank:] = jnp.where(rows == lanes, 1.0, 0.0)
    for base in range(0, rank, 8):
        left = work[base:base + 8, :rank]
        block = {}
        for j in range(8):
            column = jnp.broadcast_to(left[:, base + j:base + j + 1], (8, rank))
            for i in range(j, 8):
                block[i, j] = column[i:i + 1, :]
        a = [work[base + i:base + i + 1, :rank] for i in range(8)]
        e = [work[base + i:base + i + 1, rank:] for i in range(8)]
        for j in range(8):
            scale = lax.rsqrt(block[j, j])
            a[j] = a[j] * scale
            e[j] = e[j] * scale
            factor = {i: block[i, j] * scale for i in range(j + 1, 8)}
            for i in range(j + 1, 8):
                for k in range(j + 1, i + 1):
                    block[i, k] = block[i, k] - factor[i] * factor[k]
                a[i] = a[i] - factor[i] * a[j]
                e[i] = e[i] - factor[i] * e[j]
            work[base + j:base + j + 1, :rank] = a[j]
            work[base + j:base + j + 1, rank:] = e[j]
        if base + 8 < rank:
            high, middle, low = thirds(work[base:base + 8, :])
            first = jnp.concatenate([high, high, middle, middle, high, low], axis=0)[:, :rank]
            second = jnp.concatenate([high, middle, high, middle, low, high], axis=0)
            update = lax.dot_general(
                first, second, (((0,), (0,)), ((), ())), preferred_element_type=jnp.float32
            )
            work[base + 8:, :] = work[base + 8:, :] - update[base + 8:, :]
    out_ref[...] = jnp.where(lanes <= rows, work[:, rank:], 0.0)


def inverse_of(packed):
    rank = packed.shape[1]
    return pl.pallas_call(
        inverse_kernel,
        in_specs=[vmem()],
        out_specs=vmem(),
        out_shape=jax.ShapeDtypeStruct((rank, rank), jnp.float32),
        scratch_shapes=[pltpu.VMEM((rank, 2 * rank), jnp.float32)],
        compiler_params=params(8),
        cost_estimate=little,
        name="inverse",
    )(packed)


def onward_kernel(axis, keep_ref, got_ref, out_ref):
    half = out_ref.shape[1]
    here = pl.ds(pl.multiple_of((1 - place()[axis]) * half, 128), half)
    out_ref[...] = keep_ref[:, here] + got_ref[:, here]


def onward(axis, keep, got):
    rank, width = keep.shape
    return pl.pallas_call(
        functools.partial(onward_kernel, axis),
        in_specs=[vmem()] * 2,
        out_specs=vmem(),
        out_shape=jax.ShapeDtypeStruct((rank, width // 2), jnp.float32),
        compiler_params=params(8),
        name="onward",
    )(keep, got)


def project_kernel(n, inverse_ref, keep_x, got_x, then_x, keep_y, got_y, then_y, *refs):
    outs, ordered = refs[:-1], refs[-1]
    group, half = outs[0].shape[0], then_x.shape[1]
    each = ordered.shape[0] // n
    x, y, me = place()
    for i in range(n):
        ordered[i * each:(i + 1) * each, :] = inverse_ref[pl.ds((me ^ i) * each, each), :]
    at_x = pl.ds(pl.multiple_of(y * half, 128), half)
    at_y = pl.ds(pl.multiple_of(x * half, 128), half)
    left = (keep_x[:, at_x] + got_x[:, at_x]) + then_x[...]
    right = (keep_y[:, at_y] + got_y[:, at_y]) + then_y[...]
    left = jnp.dot(ordered[...], left, precision=precise, preferred_element_type=jnp.float32)
    right = jnp.dot(ordered[...], right, precision=precise, preferred_element_type=jnp.float32)
    for k, out in enumerate(outs):
        out[:, :half] = left[k * group:(k + 1) * group]
        out[:, half:] = right[k * group:(k + 1) * group]


def project(n, inverse, *parts):
    rank, half = parts[2].shape
    groups = n // 4
    shape = jax.ShapeDtypeStruct((rank // groups, 2 * half), jnp.float32)
    return pl.pallas_call(
        functools.partial(project_kernel, n),
        in_specs=[vmem()] * 7,
        out_specs=[vmem()] * groups,
        out_shape=[shape] * groups,
        scratch_shapes=[pltpu.VMEM((rank, rank), jnp.float32)],
        compiler_params=params(8),
        name="project",
    )(inverse, *parts)


def collect_kernel(parts, *refs):
    outs = refs[parts:]
    each = outs[0].shape[0]
    for k, out in enumerate(outs):
        total = refs[0][k * each:(k + 1) * each, :]
        for ref in refs[1:parts]:
            total = total + ref[k * each:(k + 1) * each, :]
        out[...] = total


def collect(*parts):
    group, width = parts[0].shape
    return pl.pallas_call(
        functools.partial(collect_kernel, len(parts)),
        in_specs=[vmem()] * len(parts),
        out_specs=[vmem()] * 4,
        out_shape=[jax.ShapeDtypeStruct((group // 4, width), jnp.float32)] * 4,
        compiler_params=params(8),
        name="collect",
    )(*parts)


def assemble_kernel(*refs):
    out = refs[-1]
    half = out.shape[1] // 8
    x, y = place()[:2]
    for k, ref in enumerate(refs[:-1]):
        qx, qy = x ^ (k & 1), y ^ (k >> 1)
        out[:, pl.ds(pl.multiple_of((2 * qx + qy) * half, 128), half)] = ref[:, :half]
        out[:, pl.ds(pl.multiple_of((4 + 2 * qy + qx) * half, 128), half)] = ref[:, half:]


def assemble(*blocks):
    each, width = blocks[0].shape
    return pl.pallas_call(
        assemble_kernel,
        in_specs=[vmem()] * 4,
        out_specs=vmem(),
        out_shape=jax.ShapeDtypeStruct((each, 4 * width), jnp.float32),
        compiler_params=params(8),
        name="assemble",
    )(*blocks)


def local(deviations, test_signs):
    rows, cols = deviations.shape
    n, n_cols = lax.axis_size("rows"), lax.axis_size("cols")
    samples = rows * n

    def swap(value, bit):
        return lax.ppermute(value, "rows", [(i, i ^ bit) for i in range(n)])

    kept, part = sketch_of(deviations, test_signs)
    step = 1
    while 2 * step < n_cols:
        part = part + lax.ppermute(part, "cols", [(i, i ^ step) for i in range(n_cols)])
        step *= 2
    other = lax.ppermute(part, "cols", [(i, i ^ step) for i in range(n_cols)])
    sketch, pair = join(part, other)

    leave = cross_of(False, pair, kept)
    stay = cross_of(True, pair, kept)

    gram = gram_of(lax.optimization_barrier((sketch, leave))[0])
    steps, beside = [4 ** i for i in range(1, n) if 4 ** i < n] + [1], [stay]
    for step in steps:
        found = [swap(gram, step * k) for k in range(1, min(4, n // step))]
        if beside:
            found, _ = lax.optimization_barrier((found, beside.pop()))
        for value in found:
            gram = gram + value
    inverse = inverse_of(gram)

    got_x, got_y = swap(leave[0], 1), swap(leave[1], 2)
    then_x = swap(onward(1, stay[0], got_x), 2)
    then_y = swap(onward(0, stay[1], got_y), 1)

    groups = project(n, inverse, stay[0], got_x, then_x, stay[1], got_y, then_y)
    basis = lax.dot_general(
        sketch, inverse, (((1,), (1,)), ((), ())),
        precision=precise, preferred_element_type=jnp.float32,
    ) * math.sqrt(samples)
    found = [swap(groups[k], 4 * k) for k in range(1, n // 4)]
    found, basis = lax.optimization_barrier((found, basis))

    blocks = collect(groups[0], *found)
    blocks = [blocks[0]] + [swap(blocks[k], k) for k in range(1, 4)]
    return (basis, assemble(*blocks))


def solution(mesh):
    return jax.shard_map(
        local,
        mesh=mesh,
        in_specs=(P("rows", "cols"), P("cols", None)),
        out_specs=(P("rows", None), P("rows", "cols")),
        check_vma=False,
    )
```

```python
import functools
import math

import jax
import jax.numpy as jnp
from jax import lax
from jax.experimental import pallas as pl
from jax.experimental.pallas import tpu as pltpu
from jax.sharding import PartitionSpec as P

SCANS = 8192

precise = lax.Precision.HIGHEST
MIB = 1 << 20
little = pl.CostEstimate(flops=1000, bytes_accessed=1000, transcendentals=0)


def split(value):
    high = value.astype(jnp.bfloat16)
    low = (value - high.astype(jnp.float32)).astype(jnp.bfloat16)
    return high, low


def dot(a, b):
    return jnp.dot(a, b, preferred_element_type=jnp.float32)


def vmem():
    return pl.BlockSpec(memory_space=pltpu.VMEM)


def place():
    me = lax.axis_index("rows")
    return me & 1, (me >> 1) & 1, me


def params(mib):
    return pltpu.CompilerParams(vmem_limit_bytes=mib * MIB)


def sketch_kernel(unit, gain, steps, depth, dev_hbm, sign_hbm, dev_ref, out_ref, sign_buf, omega, dev_sem, sign_sem):
    block = dev_ref.shape[0] // steps
    signs = pltpu.make_async_copy(sign_hbm, sign_buf, sign_sem)
    signs.start()

    def fetch(i):
        here = pl.ds(i * block, block)
        return pltpu.make_async_copy(dev_hbm.at[here, :], dev_ref.at[here, :], dev_sem.at[i])

    for i in range(depth - 1):
        fetch(i).start()
    signs.wait()
    omega[...] = (sign_buf[...].astype(jnp.float32) * unit).astype(jnp.bfloat16)
    for i in range(steps):
        if i + depth - 1 < steps:
            fetch(i + depth - 1).start()
        fetch(i).wait()
        here = slice(i * block, (i + 1) * block)
        high, low = split(dev_ref[here, :])
        out_ref[here, :] = (dot(high, omega[...]) + dot(low, omega[...])) * gain


def sketch_of(dev, signs):
    rows, cols = dev.shape
    rank = signs.shape[1]
    steps, depth = 4, 3
    unit = 2.0 ** -math.ceil(math.log2(math.sqrt(SCANS)))
    gain = 1.0 / (math.sqrt(SCANS) * unit)
    dev = pltpu.with_memory_space_constraint(dev, pltpu.HBM)
    signs = pltpu.with_memory_space_constraint(signs, pltpu.HBM)
    return pl.pallas_call(
        functools.partial(sketch_kernel, unit, gain, steps, depth),
        in_specs=[pl.BlockSpec(memory_space=pltpu.HBM)] * 2,
        out_specs=[vmem()] * 2,
        out_shape=[pltpu.VMEM((rows, cols), jnp.float32), pltpu.VMEM((rows, rank), jnp.float32)],
        scratch_shapes=[
            pltpu.VMEM((cols, rank), jnp.int32),
            pltpu.VMEM((cols, rank), jnp.bfloat16),
            pltpu.SemaphoreType.DMA((steps,)),
            pltpu.SemaphoreType.DMA,
        ],
        compiler_params=params(24),
        name="sketch",
    )(dev, signs)


def join_kernel(parts, *refs):
    total_ref, pair_ref = refs[parts:]
    total = refs[0][...]
    for ref in refs[1:parts]:
        total = total + ref[...]
    total_ref[...] = total
    high, low = split(total.T)
    rank = high.shape[0]
    pair_ref[:rank, :] = high
    pair_ref[rank:, :] = low


def join(*sketches):
    rows, rank = sketches[0].shape
    return pl.pallas_call(
        functools.partial(join_kernel, len(sketches)),
        in_specs=[vmem()] * len(sketches),
        out_specs=[vmem()] * 2,
        out_shape=[
            jax.ShapeDtypeStruct((rows, rank), jnp.float32),
            jax.ShapeDtypeStruct((2 * rank, rows), jnp.bfloat16),
        ],
        compiler_params=params(8),
        name="join",
    )(*sketches)


def places(shape):
    return lax.broadcasted_iota(jnp.int32, shape, 0), lax.broadcasted_iota(jnp.int32, shape, 1)


def gram_kernel(pair_ref, packed_ref):
    four = lax.dot_general(
        pair_ref[...], pair_ref[...], (((1,), (1,)), ((), ())), preferred_element_type=jnp.float32
    )
    rank = four.shape[0] // 2
    gram = (four[:rank, :rank] + four[rank:, rank:]) + (four[:rank, rank:] + four[rank:, :rank])
    half = rank // 2
    last = pltpu.roll(gram[half:], half, 1)
    rows, lanes = places(last.shape)
    packed_ref[:half, :] = jnp.where(rows <= lanes, gram[:half], last)
    diagonal = jnp.sum(jnp.where(rows == lanes, last, 0.0), axis=0, keepdims=True)
    packed_ref[half:, :] = jnp.broadcast_to(diagonal, (8, last.shape[1]))


def gram_of(pair):
    rank = pair.shape[0] // 2
    return pl.pallas_call(
        gram_kernel,
        in_specs=[vmem()],
        out_specs=vmem(),
        out_shape=jax.ShapeDtypeStruct((rank // 2 + 8, rank), jnp.float32),
        compiler_params=params(8),
        cost_estimate=little,
        name="gram",
    )(pair)


def cross_kernel(block, stay, pair_ref, dev_ref, *outs):
    rank, width = outs[0].shape
    x, y = place()[:2]
    chunks = (x, 2 + y) if stay else (1 - x, 3 - y)
    for chunk, out in zip(chunks, outs):
        for t in range(width // block):
            start = pl.multiple_of(chunk * width + t * block, 128)
            high, low = split(dev_ref[:, pl.ds(start, block)])
            both = dot(pair_ref[...], high)
            out[:, t * block:(t + 1) * block] = (both[:rank] + both[rank:]) + dot(pair_ref[:rank, :], low)


def cross_of(stay, pair, dev):
    rank, rows = pair.shape[0] // 2, pair.shape[1]
    width = dev.shape[1] // 4
    return pl.pallas_call(
        functools.partial(cross_kernel, min(512, width), stay),
        in_specs=[vmem()] * 2,
        out_specs=[vmem()] * 2,
        out_shape=[jax.ShapeDtypeStruct((rank, width), jnp.float32)] * 2,
        compiler_params=params(8),
        cost_estimate=little,
        name="cross_stay" if stay else "cross_leave",
    )(pair, dev)


def thirds(value):
    high = value.astype(jnp.bfloat16)
    rest = value - high.astype(jnp.float32)
    middle = rest.astype(jnp.bfloat16)
    low = (rest - middle.astype(jnp.float32)).astype(jnp.bfloat16)
    return high, middle, low


def inverse_kernel(packed_ref, out_ref, work):
    rank = packed_ref.shape[1]
    half = rank // 2
    packed = packed_ref[:half, :]
    rows, lanes = places(packed.shape)
    corner = jnp.where(lanes < half, packed, 0.0)
    turned = jnp.concatenate([corner, jnp.zeros_like(corner)], axis=0).T[:half]
    work[:half, :rank] = jnp.where(rows <= lanes, packed, turned)
    last = jnp.where(rows > lanes, packed, jnp.where(rows < lanes, turned, packed_ref[half:half + 1, :]))
    work[half:, :rank] = jnp.where(lanes < half, 0.0, pltpu.roll(last, half, 1))
    rows, lanes = places((rank, rank))
    work[:, rank:] = jnp.where(rows == lanes, 1.0, 0.0)
    for base in range(0, rank, 8):
        left = work[base:base + 8, :rank]
        block = {}
        for j in range(8):
            column = jnp.broadcast_to(left[:, base + j:base + j + 1], (8, rank))
            for i in range(j, 8):
                block[i, j] = column[i:i + 1, :]
        a = [work[base + i:base + i + 1, :rank] for i in range(8)]
        e = [work[base + i:base + i + 1, rank:] for i in range(8)]
        for j in range(8):
            scale = lax.rsqrt(block[j, j])
            a[j] = a[j] * scale
            e[j] = e[j] * scale
            factor = {i: block[i, j] * scale for i in range(j + 1, 8)}
            for i in range(j + 1, 8):
                for k in range(j + 1, i + 1):
                    block[i, k] = block[i, k] - factor[i] * factor[k]
                a[i] = a[i] - factor[i] * a[j]
                e[i] = e[i] - factor[i] * e[j]
            work[base + j:base + j + 1, :rank] = a[j]
            work[base + j:base + j + 1, rank:] = e[j]
        if base + 8 < rank:
            high, middle, low = thirds(work[base:base + 8, :])
            first = jnp.concatenate([high, high, middle, middle, high, low], axis=0)[:, :rank]
            second = jnp.concatenate([high, middle, high, middle, low, high], axis=0)
            update = lax.dot_general(
                first, second, (((0,), (0,)), ((), ())), preferred_element_type=jnp.float32
            )
            work[base + 8:, :] = work[base + 8:, :] - update[base + 8:, :]
    out_ref[...] = jnp.where(lanes <= rows, work[:, rank:], 0.0)


def inverse_of(packed):
    rank = packed.shape[1]
    return pl.pallas_call(
        inverse_kernel,
        in_specs=[vmem()],
        out_specs=vmem(),
        out_shape=jax.ShapeDtypeStruct((rank, rank), jnp.float32),
        scratch_shapes=[pltpu.VMEM((rank, 2 * rank), jnp.float32)],
        compiler_params=params(8),
        cost_estimate=little,
        name="inverse",
    )(packed)


def onward_kernel(axis, keep_ref, got_ref, out_ref):
    half = out_ref.shape[1]
    here = pl.ds(pl.multiple_of((1 - place()[axis]) * half, 128), half)
    out_ref[...] = keep_ref[:, here] + got_ref[:, here]


def onward(axis, keep, got):
    rank, width = keep.shape
    return pl.pallas_call(
        functools.partial(onward_kernel, axis),
        in_specs=[vmem()] * 2,
        out_specs=vmem(),
        out_shape=jax.ShapeDtypeStruct((rank, width // 2), jnp.float32),
        compiler_params=params(8),
        name="onward",
    )(keep, got)


def project_kernel(n, inverse_ref, keep_x, got_x, then_x, keep_y, got_y, then_y, *refs):
    outs, ordered = refs[:-1], refs[-1]
    group, half = outs[0].shape[0], then_x.shape[1]
    each = ordered.shape[0] // n
    x, y, me = place()
    for i in range(n):
        ordered[i * each:(i + 1) * each, :] = inverse_ref[pl.ds((me ^ i) * each, each), :]
    at_x = pl.ds(pl.multiple_of(y * half, 128), half)
    at_y = pl.ds(pl.multiple_of(x * half, 128), half)
    left = (keep_x[:, at_x] + got_x[:, at_x]) + then_x[...]
    right = (keep_y[:, at_y] + got_y[:, at_y]) + then_y[...]
    factor_high, factor_low = split(ordered[...])
    factor = jnp.concatenate([factor_high, factor_high, factor_low], axis=1)

    def applied(value):
        high, low = split(value)
        return dot(factor, jnp.concatenate([high, low, high], axis=0))

    left, right = applied(left), applied(right)
    for k, out in enumerate(outs):
        out[:, :half] = left[k * group:(k + 1) * group]
        out[:, half:] = right[k * group:(k + 1) * group]


def project(n, inverse, *parts):
    rank, half = parts[2].shape
    groups = n // 4
    shape = jax.ShapeDtypeStruct((rank // groups, 2 * half), jnp.float32)
    return pl.pallas_call(
        functools.partial(project_kernel, n),
        in_specs=[vmem()] * 7,
        out_specs=[vmem()] * groups,
        out_shape=[shape] * groups,
        scratch_shapes=[pltpu.VMEM((rank, rank), jnp.float32)],
        compiler_params=params(8),
        name="project",
    )(inverse, *parts)


def collect_kernel(parts, *refs):
    outs = refs[parts:]
    each = outs[0].shape[0]
    for k, out in enumerate(outs):
        total = refs[0][k * each:(k + 1) * each, :]
        for ref in refs[1:parts]:
            total = total + ref[k * each:(k + 1) * each, :]
        out[...] = total


def collect(*parts):
    group, width = parts[0].shape
    return pl.pallas_call(
        functools.partial(collect_kernel, len(parts)),
        in_specs=[vmem()] * len(parts),
        out_specs=[vmem()] * 4,
        out_shape=[jax.ShapeDtypeStruct((group // 4, width), jnp.float32)] * 4,
        compiler_params=params(8),
        name="collect",
    )(*parts)


def assemble_kernel(*refs):
    out = refs[-1]
    half = out.shape[1] // 8
    x, y = place()[:2]
    for k, ref in enumerate(refs[:-1]):
        qx, qy = x ^ (k & 1), y ^ (k >> 1)
        out[:, pl.ds(pl.multiple_of((2 * qx + qy) * half, 128), half)] = ref[:, :half]
        out[:, pl.ds(pl.multiple_of((4 + 2 * qy + qx) * half, 128), half)] = ref[:, half:]


def assemble(*blocks):
    each, width = blocks[0].shape
    return pl.pallas_call(
        assemble_kernel,
        in_specs=[vmem()] * 4,
        out_specs=vmem(),
        out_shape=jax.ShapeDtypeStruct((each, 4 * width), jnp.float32),
        compiler_params=params(8),
        name="assemble",
    )(*blocks)


def local(deviations, test_signs):
    rows, cols = deviations.shape
    n, n_cols = lax.axis_size("rows"), lax.axis_size("cols")
    samples = rows * n

    def swap(value, bit):
        return lax.ppermute(value, "rows", [(i, i ^ bit) for i in range(n)])

    kept, part = sketch_of(deviations, test_signs)
    step = 1
    while 2 * step < n_cols:
        part = part + lax.ppermute(part, "cols", [(i, i ^ step) for i in range(n_cols)])
        step *= 2
    other = lax.ppermute(part, "cols", [(i, i ^ step) for i in range(n_cols)])
    sketch, pair = join(part, other)

    leave = cross_of(False, pair, kept)
    stay = cross_of(True, pair, kept)

    gram = gram_of(lax.optimization_barrier((pair, leave))[0])
    steps, beside = [4 ** i for i in range(1, n) if 4 ** i < n] + [1], [stay]
    for step in steps:
        found = [swap(gram, step * k) for k in range(1, min(4, n // step))]
        if beside:
            found, _ = lax.optimization_barrier((found, beside.pop()))
        for value in found:
            gram = gram + value
    inverse = inverse_of(gram)

    got_x, got_y = swap(leave[0], 1), swap(leave[1], 2)
    then_x = swap(onward(1, stay[0], got_x), 2)
    then_y = swap(onward(0, stay[1], got_y), 1)

    groups = project(n, inverse, stay[0], got_x, then_x, stay[1], got_y, then_y)
    basis = lax.dot_general(
        sketch, inverse, (((1,), (1,)), ((), ())),
        precision=precise, preferred_element_type=jnp.float32,
    ) * math.sqrt(samples)
    order = sorted(range(1, n // 4), key=lambda k: (k == 1, k))
    found = [swap(groups[k], 4 * k) for k in order]
    found, basis = lax.optimization_barrier((found, basis))

    blocks = collect(groups[0], *found)
    moved = lax.optimization_barrier([swap(blocks[k], k) for k in (3, 2, 1)])
    return (basis, assemble(blocks[0], *moved[::-1]))


def solution(mesh):
    return jax.shard_map(
        local,
        mesh=mesh,
        in_specs=(P("rows", "cols"), P("cols", None)),
        out_specs=(P("rows", None), P("rows", "cols")),
        check_vma=False,
    )
```

```python
import functools
import math

import jax
import jax.numpy as jnp
from jax import lax
from jax.experimental import pallas as pl
from jax.experimental.pallas import tpu as pltpu
from jax.sharding import PartitionSpec as P

SCANS = 8192

precise = lax.Precision.HIGHEST
MIB = 1 << 20
little = pl.CostEstimate(flops=1000, bytes_accessed=1000, transcendentals=0)


def split(value):
    high = value.astype(jnp.bfloat16)
    low = (value - high.astype(jnp.float32)).astype(jnp.bfloat16)
    return high, low


def dot(a, b):
    return jnp.dot(a, b, preferred_element_type=jnp.float32)


def vmem():
    return pl.BlockSpec(memory_space=pltpu.VMEM)


def place():
    me = lax.axis_index("rows")
    return me & 1, (me >> 1) & 1, me


def params(mib):
    return pltpu.CompilerParams(vmem_limit_bytes=mib * MIB)


PARTS, DEPTH = (3, 3, 2, 4), 3


def sketch_kernel(unit, gain, dev_hbm, sign_hbm, dev_ref, omega, out_ref, sign_buf, dev_sem, sign_sem):
    unit_rows = dev_ref.shape[0] // sum(PARTS)
    bounds = [sum(PARTS[:i]) * unit_rows for i in range(len(PARTS) + 1)]
    signs = pltpu.make_async_copy(sign_hbm, sign_buf, sign_sem)
    signs.start()

    def fetch(i):
        here = pl.ds(bounds[i], bounds[i + 1] - bounds[i])
        return pltpu.make_async_copy(dev_hbm.at[here, :], dev_ref.at[here, :], dev_sem.at[i])

    for i in range(DEPTH - 1):
        fetch(i).start()
    signs.wait()
    omega[...] = (sign_buf[...].astype(jnp.float32) * unit).astype(jnp.bfloat16)
    for i in range(len(PARTS)):
        if i + DEPTH - 1 < len(PARTS):
            fetch(i + DEPTH - 1).start()
        fetch(i).wait()
        if i < len(PARTS) - 1:
            here = slice(bounds[i], bounds[i + 1])
            high, low = split(dev_ref[here, :])
            out_ref[here, :] = (dot(high, omega[...]) + dot(low, omega[...])) * gain


def last_sketch_kernel(gain, dev_ref, omega, out_ref):
    high, low = split(dev_ref[dev_ref.shape[0] - out_ref.shape[0]:, :])
    out_ref[...] = (dot(high, omega[...]) + dot(low, omega[...])) * gain


def sketch_of(dev, signs):
    rows, cols = dev.shape
    rank = signs.shape[1]
    block = rows // sum(PARTS) * PARTS[-1]
    unit = 2.0 ** -math.ceil(math.log2(math.sqrt(SCANS)))
    gain = 1.0 / (math.sqrt(SCANS) * unit)
    dev = pltpu.with_memory_space_constraint(dev, pltpu.HBM)
    signs = pltpu.with_memory_space_constraint(signs, pltpu.HBM)
    kept, omega, most = pl.pallas_call(
        functools.partial(sketch_kernel, unit, gain),
        in_specs=[pl.BlockSpec(memory_space=pltpu.HBM)] * 2,
        out_specs=[vmem()] * 3,
        out_shape=[
            pltpu.VMEM((rows, cols), jnp.float32),
            pltpu.VMEM((cols, rank), jnp.bfloat16),
            pltpu.VMEM((rows - block, rank), jnp.float32),
        ],
        scratch_shapes=[
            pltpu.VMEM((cols, rank), jnp.int32),
            pltpu.SemaphoreType.DMA((len(PARTS),)),
            pltpu.SemaphoreType.DMA,
        ],
        compiler_params=params(24),
        name="sketch",
    )(dev, signs)
    last = pl.pallas_call(
        functools.partial(last_sketch_kernel, gain),
        in_specs=[vmem()] * 2,
        out_specs=vmem(),
        out_shape=jax.ShapeDtypeStruct((block, rank), jnp.float32),
        compiler_params=params(8),
        name="last_sketch",
    )(kept, omega)
    return kept, most, last


def join_kernel(parts, *refs):
    total_ref, pair_ref = refs[parts:]
    total = refs[0][...]
    for ref in refs[1:parts]:
        total = total + ref[...]
    total_ref[...] = total
    high, low = split(total.T)
    rank = high.shape[0]
    pair_ref[:rank, :] = high
    pair_ref[rank:, :] = low


def join(*sketches):
    rows, rank = sketches[0].shape
    return pl.pallas_call(
        functools.partial(join_kernel, len(sketches)),
        in_specs=[vmem()] * len(sketches),
        out_specs=[vmem()] * 2,
        out_shape=[
            jax.ShapeDtypeStruct((rows, rank), jnp.float32),
            jax.ShapeDtypeStruct((2 * rank, rows), jnp.bfloat16),
        ],
        compiler_params=params(8),
        name="join",
    )(*sketches)


def places(shape):
    return lax.broadcasted_iota(jnp.int32, shape, 0), lax.broadcasted_iota(jnp.int32, shape, 1)


def gram_kernel(most_ref, last_ref, packed_ref):
    four = sum(
        lax.dot_general(
            ref[...], ref[...], (((1,), (1,)), ((), ())), preferred_element_type=jnp.float32
        )
        for ref in (most_ref, last_ref)
    )
    rank = four.shape[0] // 2
    gram = (four[:rank, :rank] + four[rank:, rank:]) + (four[:rank, rank:] + four[rank:, :rank])
    half = rank // 2
    last = pltpu.roll(gram[half:], half, 1)
    rows, lanes = places(last.shape)
    packed_ref[:half, :] = jnp.where(rows <= lanes, gram[:half], last)
    diagonal = jnp.sum(jnp.where(rows == lanes, last, 0.0), axis=0, keepdims=True)
    packed_ref[half:, :] = jnp.broadcast_to(diagonal, (8, last.shape[1]))


def gram_of(pair, last):
    rank = pair.shape[0] // 2
    return pl.pallas_call(
        gram_kernel,
        in_specs=[vmem()] * 2,
        out_specs=vmem(),
        out_shape=jax.ShapeDtypeStruct((rank // 2 + 8, rank), jnp.float32),
        compiler_params=params(8),
        cost_estimate=little,
        name="gram",
    )(pair, last)


def cross_kernel(block, stay, starts, *refs):
    pairs, dev_ref, prior, outs = refs[:len(starts)], refs[len(starts)], refs[len(starts) + 1:-2], refs[-2:]
    rank, width = outs[0].shape
    x, y = place()[:2]
    chunks = (x, 2 + y) if stay else (1 - x, 3 - y)
    for j, (chunk, out) in enumerate(zip(chunks, outs)):
        for t in range(width // block):
            start = pl.multiple_of(chunk * width + t * block, 128)
            here = slice(t * block, (t + 1) * block)
            value = prior[j][:, here] if prior else None
            for first, pair in zip(starts, pairs):
                high, low = split(dev_ref[first:first + pair.shape[1], pl.ds(start, block)])
                both = dot(pair[...], high)
                term = (both[:rank] + both[rank:]) + dot(pair[:rank, :], low)
                value = term if value is None else value + term
            out[:, here] = value


def cross_of(stay, pairs, dev, prior=()):
    starts, pairs = list(pairs), list(pairs.values())
    rank = pairs[0].shape[0] // 2
    width = dev.shape[1] // 4
    return pl.pallas_call(
        functools.partial(cross_kernel, min(512, width), stay, starts),
        in_specs=[vmem()] * (len(pairs) + 1 + len(prior)),
        out_specs=[vmem()] * 2,
        out_shape=[jax.ShapeDtypeStruct((rank, width), jnp.float32)] * 2,
        compiler_params=params(8),
        cost_estimate=little,
        name="cross_stay" if stay else "cross_leave",
    )(*pairs, dev, *prior)


def thirds(value):
    high = value.astype(jnp.bfloat16)
    rest = value - high.astype(jnp.float32)
    middle = rest.astype(jnp.bfloat16)
    low = (rest - middle.astype(jnp.float32)).astype(jnp.bfloat16)
    return high, middle, low


def inverse_kernel(packed_ref, out_ref, work):
    rank = packed_ref.shape[1]
    half = rank // 2
    packed = packed_ref[:half, :]
    rows, lanes = places(packed.shape)
    corner = jnp.where(lanes < half, packed, 0.0)
    turned = jnp.concatenate([corner, jnp.zeros_like(corner)], axis=0).T[:half]
    work[:half, :rank] = jnp.where(rows <= lanes, packed, turned)
    last = jnp.where(rows > lanes, packed, jnp.where(rows < lanes, turned, packed_ref[half:half + 1, :]))
    work[half:, :rank] = jnp.where(lanes < half, 0.0, pltpu.roll(last, half, 1))
    rows, lanes = places((rank, rank))
    work[:, rank:] = jnp.where(rows == lanes, 1.0, 0.0)
    for base in range(0, rank, 8):
        left = work[base:base + 8, :rank]
        block = {}
        for j in range(8):
            column = jnp.broadcast_to(left[:, base + j:base + j + 1], (8, rank))
            for i in range(j, 8):
                block[i, j] = column[i:i + 1, :]
        a = [work[base + i:base + i + 1, :rank] for i in range(8)]
        e = [work[base + i:base + i + 1, rank:] for i in range(8)]
        for j in range(8):
            scale = lax.rsqrt(block[j, j])
            a[j] = a[j] * scale
            e[j] = e[j] * scale
            factor = {i: block[i, j] * scale for i in range(j + 1, 8)}
            for i in range(j + 1, 8):
                for k in range(j + 1, i + 1):
                    block[i, k] = block[i, k] - factor[i] * factor[k]
                a[i] = a[i] - factor[i] * a[j]
                e[i] = e[i] - factor[i] * e[j]
            work[base + j:base + j + 1, :rank] = a[j]
            work[base + j:base + j + 1, rank:] = e[j]
        if base + 8 < rank:
            high, middle, low = thirds(work[base:base + 8, :])
            first = jnp.concatenate([high, high, middle, middle, high, low], axis=0)[:, :rank]
            second = jnp.concatenate([high, middle, high, middle, low, high], axis=0)
            update = lax.dot_general(
                first, second, (((0,), (0,)), ((), ())), preferred_element_type=jnp.float32
            )
            work[base + 8:, :] = work[base + 8:, :] - update[base + 8:, :]
    out_ref[...] = jnp.where(lanes <= rows, work[:, rank:], 0.0)


def inverse_of(packed):
    rank = packed.shape[1]
    return pl.pallas_call(
        inverse_kernel,
        in_specs=[vmem()],
        out_specs=vmem(),
        out_shape=jax.ShapeDtypeStruct((rank, rank), jnp.float32),
        scratch_shapes=[pltpu.VMEM((rank, 2 * rank), jnp.float32)],
        compiler_params=params(8),
        cost_estimate=little,
        name="inverse",
    )(packed)


def onward_kernel(axis, keep_ref, got_ref, out_ref):
    half = out_ref.shape[1]
    here = pl.ds(pl.multiple_of((1 - place()[axis]) * half, 128), half)
    out_ref[...] = keep_ref[:, here] + got_ref[:, here]


def onward(axis, keep, got):
    rank, width = keep.shape
    return pl.pallas_call(
        functools.partial(onward_kernel, axis),
        in_specs=[vmem()] * 2,
        out_specs=vmem(),
        out_shape=jax.ShapeDtypeStruct((rank, width // 2), jnp.float32),
        compiler_params=params(8),
        name="onward",
    )(keep, got)


def project_kernel(n, inverse_ref, keep_x, got_x, then_x, keep_y, got_y, then_y, *refs):
    outs, ordered = refs[:-1], refs[-1]
    group, half = outs[0].shape[0], then_x.shape[1]
    each = ordered.shape[0] // n
    x, y, me = place()
    for i in range(n):
        ordered[i * each:(i + 1) * each, :] = inverse_ref[pl.ds((me ^ i) * each, each), :]
    at_x = pl.ds(pl.multiple_of(y * half, 128), half)
    at_y = pl.ds(pl.multiple_of(x * half, 128), half)
    left = (keep_x[:, at_x] + got_x[:, at_x]) + then_x[...]
    right = (keep_y[:, at_y] + got_y[:, at_y]) + then_y[...]
    factor_high, factor_low = split(ordered[...])
    factor = jnp.concatenate([factor_high, factor_high, factor_low], axis=1)

    def applied(value):
        high, low = split(value)
        return dot(factor, jnp.concatenate([high, low, high], axis=0))

    left, right = applied(left), applied(right)
    for k, out in enumerate(outs):
        out[:, :half] = left[k * group:(k + 1) * group]
        out[:, half:] = right[k * group:(k + 1) * group]


def project(n, inverse, *parts):
    rank, half = parts[2].shape
    groups = n // 4
    shape = jax.ShapeDtypeStruct((rank // groups, 2 * half), jnp.float32)
    return pl.pallas_call(
        functools.partial(project_kernel, n),
        in_specs=[vmem()] * 7,
        out_specs=[vmem()] * groups,
        out_shape=[shape] * groups,
        scratch_shapes=[pltpu.VMEM((rank, rank), jnp.float32)],
        compiler_params=params(8),
        name="project",
    )(inverse, *parts)


def collect_kernel(parts, *refs):
    outs = refs[parts:]
    each = outs[0].shape[0]
    for k, out in enumerate(outs):
        total = refs[0][k * each:(k + 1) * each, :]
        for ref in refs[1:parts]:
            total = total + ref[k * each:(k + 1) * each, :]
        out[...] = total


def collect(*parts):
    group, width = parts[0].shape
    return pl.pallas_call(
        functools.partial(collect_kernel, len(parts)),
        in_specs=[vmem()] * len(parts),
        out_specs=[vmem()] * 4,
        out_shape=[jax.ShapeDtypeStruct((group // 4, width), jnp.float32)] * 4,
        compiler_params=params(8),
        name="collect",
    )(*parts)


def assemble_kernel(*refs):
    out = refs[-1]
    half = out.shape[1] // 8
    x, y = place()[:2]
    for k, ref in enumerate(refs[:-1]):
        qx, qy = x ^ (k & 1), y ^ (k >> 1)
        out[:, pl.ds(pl.multiple_of((2 * qx + qy) * half, 128), half)] = ref[:, :half]
        out[:, pl.ds(pl.multiple_of((4 + 2 * qy + qx) * half, 128), half)] = ref[:, half:]


def assemble(*blocks):
    each, width = blocks[0].shape
    return pl.pallas_call(
        assemble_kernel,
        in_specs=[vmem()] * 4,
        out_specs=vmem(),
        out_shape=jax.ShapeDtypeStruct((each, 4 * width), jnp.float32),
        compiler_params=params(8),
        name="assemble",
    )(*blocks)


def local(deviations, test_signs):
    rows, cols = deviations.shape
    n, n_cols = lax.axis_size("rows"), lax.axis_size("cols")
    samples = rows * n

    def swap(value, bit):
        return lax.ppermute(value, "rows", [(i, i ^ bit) for i in range(n)])

    def over_cols(part):
        step = 1
        while 2 * step < n_cols:
            part = part + lax.ppermute(part, "cols", [(i, i ^ step) for i in range(n_cols)])
            step *= 2
        return part, lax.ppermute(part, "cols", [(i, i ^ step) for i in range(n_cols)])

    kept, most, last = sketch_of(deviations, test_signs)
    sketch, pair = join(*over_cols(most))
    last = over_cols(last)
    tail = rows - last[0].shape[0]

    leave = cross_of(False, {0: pair}, kept)
    last, leave = lax.optimization_barrier((last, leave))
    last_sketch, last_pair = join(*last)
    leave = cross_of(False, {tail: last_pair}, kept, leave)
    stay = cross_of(True, {0: pair, tail: last_pair}, kept)

    gram = gram_of(*lax.optimization_barrier((pair, last_pair, leave))[:2])
    steps, beside = [4 ** i for i in range(1, n) if 4 ** i < n] + [1], [stay]
    for step in steps:
        found = [swap(gram, step * k) for k in range(1, min(4, n // step))]
        if beside:
            found, _ = lax.optimization_barrier((found, beside.pop()))
        for value in found:
            gram = gram + value
    inverse = inverse_of(gram)

    got_x, got_y = swap(leave[0], 1), swap(leave[1], 2)
    then_x = swap(onward(1, stay[0], got_x), 2)
    then_y = swap(onward(0, stay[1], got_y), 1)

    groups = project(n, inverse, stay[0], got_x, then_x, stay[1], got_y, then_y)
    basis = lax.dot_general(
        jnp.concatenate([sketch, last_sketch]), inverse, (((1,), (1,)), ((), ())),
        precision=precise, preferred_element_type=jnp.float32,
    ) * math.sqrt(samples)
    order = sorted(range(1, n // 4), key=lambda k: (k == 1, k))
    found = [swap(groups[k], 4 * k) for k in order]
    found, basis = lax.optimization_barrier((found, basis))

    blocks = collect(groups[0], *found)
    moved = lax.optimization_barrier([swap(blocks[k], k) for k in (3, 2, 1)])
    return (basis, assemble(blocks[0], *moved[::-1]))


def solution(mesh):
    return jax.shard_map(
        local,
        mesh=mesh,
        in_specs=(P("rows", "cols"), P("cols", None)),
        out_specs=(P("rows", None), P("rows", "cols")),
        check_vma=False,
    )
```
